32 devices in a mesh: feat: 4 (over x, core), work: 8 (over z, y).
Axes of the slice: x: 2, y: 2, z: 4, core: 2. Of those that a mesh axis runs over, the one named last changes fastest.
Arguments:
- momentum: bfloat16 [8, 8192, 1024], P('work', 'feat'), may hold values from -6 to 6
- gradient: bfloat16 [8, 8192, 1024], P('work', 'feat'), may hold values from -6 to 6
- weight: bfloat16 [8192, 1024], P('feat'), may hold values from -3 to 3
- tokens: bfloat16 [8192, 8192], P('work', 'feat'), may hold values from -6 to 6
- select: int32 [8, 64, 8, 4], P('work', 'feat'), may hold values from 0 to 127, as said below
Outputs:
- moment_out: bfloat16 [8, 8192, 1024], P('work', 'feat')
- weight_out: bfloat16 [8192, 1024], P('feat')
- projected: bfloat16 [8192, 1024], P('work', 'feat')
The draws below stay inside these ranges and needn't reach their ends.
Inputs may be any that keep to these rules, and one draw needn't show every extreme that they name: `select`: for each worker and tile the 4 indices are distinct.
All inputs are finite; a program needn't handle non-finite values.
Results may differ from the reference program's by a relative error of at most 0.015.
Values may be sent and summed in bfloat16 or wider, within the bound.
A program may use at most 128 MiB of HBM per device.

```python
import math
import jax
import jax.numpy as jnp
from jax import lax

D = 8192
KV = 1024
TILE = 128
KEEP = 4
WORKERS = 8
TOKENS = 8192


def draw_select(key, part):
    scores = jax.random.randint(key, (WORKERS, D // TILE, KV // TILE, TILE), 0, 1048576)
    scores = scores * TILE + jnp.arange(TILE, dtype=jnp.int32)
    return lax.top_k(scores, KEEP)[1].astype(jnp.int32)


def block_scale(own_key, dims, pieces, least, high):
    loudness, own = 1.0, jax.random.fold_in(own_key, 6)
    for position, parts in pieces:
        draws = jnp.exp(jax.random.uniform(jax.random.fold_in(own, position), (parts,), jnp.float32, least / len(pieces), high / len(pieces)))
        loudness = loudness * jnp.repeat(draws, dims[position] // parts).reshape([-1 if axis == position else 1 for axis in range(len(dims))])
    return loudness


def bell_draw(rng, extent, deviation, bound, split=(), held_as=jnp.bfloat16):
    values = deviation * jax.random.normal(rng, extent, jnp.float32)
    if split:
        values = values * block_scale(rng, extent, split, -0.22, 0.18)
    return jnp.clip(values, -bound, bound).astype(held_as)


def setup_inputs(seed: int = 0) -> dict:
    arg_keys = jax.random.split(jax.random.key(seed), 6)
    return {
        "momentum": bell_draw(arg_keys[0], (WORKERS, D, KV), 1.0, 6.0, ((0, 8), (1, 4))),
        "gradient": bell_draw(arg_keys[1], (WORKERS, D, KV), 1.0, 6.0, ((0, 8), (1, 4))),
        "weight": bell_draw(arg_keys[2], (D, KV), 0.5, 3.0, ((0, 4),)),
        "tokens": bell_draw(arg_keys[3], (TOKENS, D), 1.0, 6.0, ((0, 8), (1, 4))),
        "select": draw_select(jax.random.fold_in(arg_keys[5], 71), 0),
    }


HIGHEST_PRECISION = lax.Precision.HIGHEST
DECAY = 0.9
RATE = 8.0

def cosine_basis(order):
    freq = jnp.arange(order, dtype=jnp.int32).astype(jnp.float32)[:, None]
    place = jnp.arange(order, dtype=jnp.int32).astype(jnp.float32)[None, :]
    scale = jnp.where(freq == 0.0, math.sqrt(1.0 / order), math.sqrt(2.0 / order))
    return (scale * jnp.cos(math.pi * (2.0 * place + 1.0) * freq / (2.0 * order))).astype(jnp.float32)

def reference(momentum, gradient, weight, tokens, select):
    basis = cosine_basis(TILE)
    row_tiles = D // TILE
    col_tiles = KV // TILE
    positions = jnp.arange(TILE, dtype=jnp.int32)

    def worker_step(running, inputs):
        moment, grad, chosen = inputs
        blended = (DECAY * moment.astype(jnp.float32) + grad.astype(jnp.float32)).reshape(row_tiles, TILE, col_tiles, TILE)
        onehot = (chosen[..., None] == positions).astype(jnp.float32)
        rows_basis = jnp.einsum('abkr,rj->abkj', onehot, basis, precision=HIGHEST_PRECISION)
        halfway = jnp.einsum('abkr,arbc->abkc', rows_basis, blended, precision=HIGHEST_PRECISION)
        coeffs = jnp.einsum('abkc,jc->abkj', halfway, basis, precision=HIGHEST_PRECISION)
        partial_value = jnp.einsum('abkj,jc->abkc', coeffs, basis, precision=HIGHEST_PRECISION)
        decoded = jnp.einsum('abkr,abkc->arbc', rows_basis, partial_value, precision=HIGHEST_PRECISION)
        residual = (blended - decoded).reshape(D, KV).astype(jnp.bfloat16)
        placed = jnp.einsum('abkr,abkj->arbj', onehot, coeffs, precision=HIGHEST_PRECISION)
        return (running + placed, residual)
    initial = jnp.zeros((row_tiles, TILE, col_tiles, TILE), jnp.float32)
    summed, moment_out = lax.scan(worker_step, initial, (momentum, gradient, select))
    average = summed / WORKERS
    left_side = jnp.einsum('rj,arbc->ajbc', basis, average, precision=HIGHEST_PRECISION)
    update = jnp.einsum('ajbc,cd->ajbd', left_side, basis, precision=HIGHEST_PRECISION).reshape(D, KV)
    weight_out = (weight.astype(jnp.float32) - RATE * update).astype(jnp.bfloat16)
    projected = (jnp.dot(tokens, weight_out, preferred_element_type=jnp.float32) * (1.0 / math.sqrt(D))).astype(jnp.bfloat16)
    return (moment_out, weight_out, projected)
```

```python
import functools
import math

import jax
import jax.numpy as jnp
import ml_dtypes
import numpy as np
from jax import lax
from jax.experimental import pallas as pl
from jax.experimental.pallas import tpu as pltpu
from jax.sharding import PartitionSpec as P

TILE = 128
GROUP = 4
DECAY = 0.9
RATE = 8.0
BF16 = jnp.bfloat16
F32 = jnp.float32
MESH = pl.DeviceIdType.MESH


def cosine_basis():
    k = np.arange(TILE)[:, None].astype(np.float64)
    n = np.arange(TILE)[None, :].astype(np.float64)
    scale = np.where(k == 0, math.sqrt(1.0 / TILE), math.sqrt(2.0 / TILE))
    return scale * np.cos(math.pi * (2.0 * n + 1.0) * k / (2.0 * TILE))


def dot(a, b):
    return jnp.dot(a, b, preferred_element_type=F32)


def dot_nt(a, b):
    return lax.dot_general(a, b, (((1,), (1,)), ((), ())), preferred_element_type=F32)


def encode_kernel(nq, m_ref, g_ref, s_ref, basis_ref, basis_t_ref, out_ref, pv_ref, so_ref):
    step = pl.program_id(0)
    cols = m_ref.shape[2]
    ctiles = s_ref.shape[2]
    keep = s_ref.shape[3]
    per = keep * ctiles
    lane = lax.broadcasted_iota(jnp.int32, (ctiles, TILE), 1)

    @pl.when(step == 0)
    def _():
        so_ref[...] = jnp.zeros_like(so_ref)

    marks = []
    listed = so_ref[...]
    for i in range(GROUP):
        chosen = s_ref[0, i]
        for k in range(keep):
            wide = jnp.broadcast_to(chosen[:, k : k + 1], (ctiles, TILE))
            marks.append((wide == lane).astype(F32))
            listed = jnp.where(lane == (step * GROUP + i) * keep + k, wide.astype(F32), listed)
    so_ref[...] = listed
    onehot = jnp.concatenate(marks, axis=0).astype(BF16)
    rows = dot(onehot, basis_ref[...]).astype(BF16)
    rows_t = dot_nt(basis_t_ref[...], onehot).astype(BF16)

    row_id = lax.broadcasted_iota(jnp.int32, (per, cols), 0)
    col_id = lax.broadcasted_iota(jnp.int32, (per, cols), 1)
    own_tile = (row_id & (ctiles - 1)) == (col_id >> 7)
    kept = []
    for i in range(GROUP):
        at = slice(i * TILE, (i + 1) * TILE)
        blended = DECAY * m_ref[0, at].astype(F32) + g_ref[0, at].astype(F32)
        part = dot(rows[i * per : (i + 1) * per], blended.astype(BF16))
        kept.append(jnp.where(own_tile, part, 0.0).astype(BF16))
    kept = jnp.concatenate(kept, axis=0)

    fold_r = lax.broadcasted_iota(jnp.int32, (GROUP * keep, GROUP * per), 0)
    fold_c = lax.broadcasted_iota(jnp.int32, (GROUP * keep, GROUP * per), 1)
    fold = (fold_r == fold_c // ctiles).astype(F32).astype(BF16)
    compact = dot(fold, kept).astype(BF16)
    for c in range(ctiles):
        owner, q = c // nq, c % nq
        pv_ref[(owner // 2) * nq + q, owner % 2] = compact[:, c * TILE : (c + 1) * TILE]

    own_lane = lax.broadcasted_iota(jnp.int32, (TILE, GROUP * per), 1) // per
    for i in range(GROUP):
        at = slice(i * TILE, (i + 1) * TILE)
        blended = DECAY * m_ref[0, at].astype(F32) + g_ref[0, at].astype(F32)
        lhs = jnp.where(own_lane == i, rows_t, jnp.zeros_like(rows_t))
        out_ref[0, at] = (blended - dot(lhs, kept)).astype(BF16)


def mix_kernel(
    xs_n, ys_n, zs_n, nq, scale, feature_scale,
    pv_ref, so_ref, w_ref, t_ref, basis_t_ref,
    wout_ref, proj_ref,
    gat, selg, ohs, bsel, wv, tv, wo, own, cs, cr, xsend, xr,
    w_sem, t_sem, wo_sem, loc_sem, ag_send, ag_recv, c_send, c_recv, x_send, x_recv,
):
    feat, work = lax.axis_index("feat"), lax.axis_index("work")
    x, core = feat // 2, feat % 2
    z, y = work // ys_n, work % ys_n
    workers = ys_n * zs_n
    steps = xs_n * nq
    ak = gat.shape[3]
    groups = ak // 16
    span = workers * 16
    tokens = tv.shape[0]
    half = tokens // 2
    width = GROUP * TILE

    def zpeer(d):
        return lax.rem(z + d, zs_n) * ys_n + y

    def ypeer(d):
        return z * ys_n + lax.rem(y + d, ys_n)

    other_core = x * 2 + 1 - core

    def xpeer(d):
        return lax.rem(x + d, xs_n) * 2 + core

    def owner_x(s):
        return lax.rem(x + 1 + s // nq, xs_n)

    def tile_of(s, h):
        cc = core if h == 0 else 1 - core
        return (owner_x(s) * 2 + cc) * nq + s % nq

    loads = []
    for s in range(steps):
        for h in range(2):
            off = pl.multiple_of(tile_of(s, h) * TILE, TILE)
            loads.append(
                pltpu.make_async_copy(w_ref.at[:, pl.ds(off, TILE)], wv.at[s, h], w_sem.at[s, h])
            )
    load_t = pltpu.make_async_copy(t_ref, tv, t_sem.at[0])
    for s in range(steps + 1):
        src = so_ref if s == 0 else pv_ref.at[owner_x(s - 1) * nq + (s - 1) % nq]
        dst = selg.at[work] if s == 0 else gat.at[s - 1, work]
        pltpu.make_async_copy(src, dst, loc_sem.at[s]).start()

    barrier = pltpu.get_barrier_semaphore()
    count = 0
    for d in range(1, zs_n):
        pl.semaphore_signal(barrier, inc=1, device_id={"work": zpeer(d)}, device_id_type=MESH)
        count += 1
    for d in range(1, ys_n):
        pl.semaphore_signal(barrier, inc=1, device_id={"work": ypeer(d)}, device_id_type=MESH)
        count += 1
    pl.semaphore_signal(barrier, inc=1, device_id={"feat": other_core}, device_id_type=MESH)
    count += 1
    for d in range(1, xs_n):
        pl.semaphore_signal(barrier, inc=1, device_id={"feat": xpeer(d)}, device_id_type=MESH)
        count += 1
    pl.semaphore_wait(barrier, count)

    def source(r):
        return so_ref if r == 0 else pv_ref.at[owner_x(r - 1) * nq + (r - 1) % nq]

    def slot(r, w):
        return selg.at[w] if r == 0 else gat.at[r - 1, w]

    sent = []

    def push(r, src, w, to, which):
        copy = pltpu.make_async_remote_copy(
            src_ref=src, dst_ref=slot(r, w),
            send_sem=ag_send.at[r, which], recv_sem=ag_recv.at[r, w],
            device_id={"work": to}, device_id_type=MESH,
        )
        copy.start()
        sent.append(copy)

    def arrived(r, w):
        pltpu.make_async_remote_copy(
            src_ref=slot(r, w), dst_ref=slot(r, w),
            send_sem=ag_send.at[r, 0], recv_sem=ag_recv.at[r, w],
            device_id={"work": work}, device_id_type=MESH,
        ).wait_recv()

    def push_own(r):
        for d in range(1, zs_n):
            push(r, source(r), work, zpeer(d), d - 1)
        for e in range(1, ys_n):
            push(r, source(r), work, ypeer(e), zs_n - 1 + e - 1)

    def forward(r):
        base = zs_n - 1 + ys_n - 1
        for d in range(1, zs_n):
            w = zpeer(d)
            arrived(r, w)
            for e in range(1, ys_n):
                push(r, slot(r, w), w, ypeer(e), base + (d - 1) * (ys_n - 1) + e - 1)

    def rest(r):
        for e in range(1, ys_n):
            for d in range(zs_n):
                arrived(r, lax.rem(z + d, zs_n) * ys_n + lax.rem(y + e, ys_n))
        pltpu.make_async_copy(source(r), slot(r, work), loc_sem.at[r]).wait()

    for r in range(steps + 1):
        push_own(r)
    load_t.start()
    for copy in loads:
        copy.start()
    forward(0)
    forward(1)
    rest(0)

    ctiles = selg.shape[1]
    table = selg[...].reshape(workers * ctiles, TILE)
    fill = -table.shape[0] % TILE
    if fill:
        table = jnp.concatenate([table, jnp.zeros((fill, TILE), F32)], axis=0)
    table = table.T[:ak]
    lane = lax.broadcasted_iota(jnp.int32, (ak, TILE), 1).astype(F32)
    for w in range(workers):
        for c in range(ctiles):
            at = w * ctiles + c
            wide = jnp.broadcast_to(table[:, at : at + 1], (ak, TILE))
            hot = (wide == lane).astype(F32).astype(BF16)
            ohs[c, :, w * 16 : (w + 1) * 16, :] = hot.reshape(groups, 16, TILE)
    for c in range(ctiles):
        for g in range(groups):
            bsel[c, g] = dot_nt(basis_t_ref[...], ohs[c, g]).astype(BF16)

    part_of = (lax.broadcasted_iota(jnp.int32, (TILE, span), 1) >> 2) & (GROUP - 1)

    def decode(s):
        for h in range(2):
            cc = core if h == 0 else 1 - core
            c = tile_of(s, h)
            loads[s * 2 + h].wait()

            def body(g, carry):
                r16 = pl.multiple_of(g * 16, 16)
                rw = pl.multiple_of(g * width, width)
                values = gat[s, :, cc, pl.ds(r16, 16), :].reshape(span, TILE)
                vectors = bsel[c, g]
                lhs = jnp.concatenate(
                    [jnp.where(part_of == i, vectors, jnp.zeros_like(vectors)) for i in range(GROUP)],
                    axis=0,
                )
                update = dot(lhs, values)
                fresh = wv[s, h, pl.ds(rw, width), :].astype(F32) - scale * update
                wo[s, pl.ds(rw, width), h * TILE : (h + 1) * TILE] = fresh.astype(BF16)
                return carry

            lax.fori_loop(0, groups, body, 0)
            out_copy(s, h).start()

    def out_copy(s, h):
        off = pl.multiple_of(tile_of(s, h) * TILE, TILE)
        return pltpu.make_async_copy(
            wo.at[s, :, h * TILE : (h + 1) * TILE], wout_ref.at[:, pl.ds(off, TILE)], wo_sem.at[s, h]
        )

    def core_copy(s, p):
        at = slice(p * half, (p + 1) * half)
        return pltpu.make_async_remote_copy(
            src_ref=cs.at[s, at], dst_ref=cr.at[s, at],
            send_sem=c_send.at[s, p], recv_sem=c_recv.at[s, p],
            device_id={"feat": other_core}, device_id_type=MESH,
        )

    def x_copy(s, p):
        d = s // nq + 1
        at = slice(p * half, (p + 1) * half)
        return pltpu.make_async_remote_copy(
            src_ref=xsend.at[s, at], dst_ref=xr.at[s, at],
            send_sem=x_send.at[s, p], recv_sem=x_recv.at[s, p],
            device_id={"feat": xpeer(d)}, device_id_type=MESH,
        )

    block = min(256, half)

    def multiply(s, p):
        def body(t, carry):
            at = pl.ds(pl.multiple_of(p * half + t * block, block), block)
            both = dot(tv[at, :], wo[s])
            own[s, at, :] = both[:, :TILE]
            cs[s, at, :] = both[:, TILE:].astype(BF16)
            return carry

        lax.fori_loop(0, half // block, body, 0)
        core_copy(s, p).start()

    away = steps - nq

    def finish(s, p):
        at = slice(p * half, (p + 1) * half)
        core_copy(s, p).wait_recv()
        xsend[s, at] = (own[s, at] + cr[s, at].astype(F32)).astype(BF16)
        x_copy(s, p).start()

    for s in range(steps):
        rest(s + 1)
        decode(s)
        if s + 2 <= steps:
            forward(s + 2)
        if s == 0:
            load_t.wait()
        for p in range(2):
            multiply(s, p)
        if s < away:
            for p in range(2):
                finish(s, p)

    for q in range(nq):
        s = away + q
        for p in range(2):
            at = slice(p * half, (p + 1) * half)
            core_copy(s, p).wait_recv()
            total = own[s, at] + cr[s, at].astype(F32)
            for d in range(xs_n - 1):
                x_copy(d * nq + q, p).wait_recv()
                total = total + xr[d * nq + q, at].astype(F32)
            proj_ref[at, q * TILE : (q + 1) * TILE] = (total * feature_scale).astype(BF16)

    for copy in sent:
        copy.wait_send()
    for s in range(steps):
        for p in range(2):
            core_copy(s, p).wait_send()
            if s < away:
                x_copy(s, p).wait_send()
        for h in range(2):
            out_copy(s, h).wait()


def local(feats, momentum, gradient, weight, tokens, select):
    workers = lax.axis_size("work")
    rows, cols = weight.shape
    row_tiles, ctiles, keep = select.shape[1:]
    nq = ctiles // feats
    xs_n = feats // 2
    ys_n = xs_n if workers % xs_n == 0 else 1
    zs_n = workers // ys_n
    steps = xs_n * nq
    ak = row_tiles * keep
    count = tokens.shape[0]
    basis = cosine_basis()
    basis_c = jnp.asarray(basis.astype(ml_dtypes.bfloat16))
    basis_t = jnp.asarray(np.ascontiguousarray(basis.T).astype(ml_dtypes.bfloat16))
    height = GROUP * TILE

    moment_out, values, listed = pl.pallas_call(
        functools.partial(encode_kernel, nq),
        grid=(row_tiles // GROUP,),
        in_specs=[
            pl.BlockSpec((1, height, cols), lambda g: (0, g, 0)),
            pl.BlockSpec((1, height, cols), lambda g: (0, g, 0)),
            pl.BlockSpec((1, GROUP, ctiles, keep), lambda g: (0, g, 0, 0)),
            pl.BlockSpec((TILE, TILE), lambda g: (0, 0)),
            pl.BlockSpec((TILE, TILE), lambda g: (0, 0)),
        ],
        out_specs=[
            pl.BlockSpec((1, height, cols), lambda g: (0, g, 0)),
            pl.BlockSpec((steps, 2, 16, TILE), lambda g: (0, 0, g, 0)),
            pl.BlockSpec((ctiles, TILE), lambda g: (0, 0)),
        ],
        out_shape=[
            jax.ShapeDtypeStruct(momentum.shape, BF16),
            jax.ShapeDtypeStruct((steps, 2, ak, TILE), BF16),
            jax.ShapeDtypeStruct((ctiles, TILE), F32),
        ],
        compiler_params=pltpu.CompilerParams(vmem_limit_bytes=30 * 1024 * 1024),
        cost_estimate=pl.CostEstimate(flops=4 * rows * cols * 160, bytes_accessed=6 * rows * cols, transcendentals=0),
        name="encode",
    )(momentum, gradient, select, basis_c, basis_t)

    sends = (zs_n - 1) + zs_n * (ys_n - 1)
    away = steps - nq
    dma = pltpu.SemaphoreType.DMA
    anywhere = pl.BlockSpec(memory_space=pl.ANY)
    vmem = pl.BlockSpec(memory_space=pltpu.VMEM)
    weight_out, projected = pl.pallas_call(
        functools.partial(
            mix_kernel, xs_n, ys_n, zs_n, nq, RATE / workers, 1.0 / math.sqrt(rows * feats)
        ),
        in_specs=[anywhere, anywhere, anywhere, anywhere, vmem],
        out_specs=[anywhere, vmem],
        out_shape=[
            jax.ShapeDtypeStruct(weight.shape, BF16),
            jax.ShapeDtypeStruct((count, cols // feats), BF16),
        ],
        scratch_shapes=[
            pltpu.VMEM((steps, workers, 2, ak, TILE), BF16),
            pltpu.VMEM((workers, ctiles, TILE), F32),
            pltpu.VMEM((ctiles, ak // 16, workers * 16, TILE), BF16),
            pltpu.VMEM((ctiles, ak // 16, TILE, workers * 16), BF16),
            pltpu.VMEM((steps, 2, rows, TILE), BF16),
            pltpu.VMEM((count, rows), BF16),
            pltpu.VMEM((steps, rows, 2 * TILE), BF16),
            pltpu.VMEM((steps, count, TILE), F32),
            pltpu.VMEM((steps, count, TILE), BF16),
            pltpu.VMEM((steps, count, TILE), BF16),
            pltpu.VMEM((away, count, TILE), BF16),
            pltpu.VMEM((away, count, TILE), BF16),
            dma((steps, 2)),
            dma((1,)),
            dma((steps, 2)),
            dma((steps + 1,)),
            dma((steps + 1, sends)),
            dma((steps + 1, workers)),
            dma((steps, 2)),
            dma((steps, 2)),
            dma((away, 2)),
            dma((away, 2)),
        ],
        compiler_params=pltpu.CompilerParams(
            collective_id=0, has_side_effects=True, vmem_limit_bytes=40 * 1024 * 1024
        ),
        cost_estimate=pl.CostEstimate(
            flops=2 * count * rows * cols, bytes_accessed=20 * 1024 * 1024, transcendentals=0
        ),
        name="mix",
    )(values, listed, weight, tokens, basis_t)
    return (moment_out, weight_out, projected)


def solution(mesh):
    in_specs = (
        P("work", "feat", None),
        P("work", "feat", None),
        P("feat", None),
        P("work", "feat"),
        P("work", "feat", None, None),
    )
    out_specs = (P("work", "feat", None), P("feat", None), P("work", "feat"))
    return jax.shard_map(
        functools.partial(local, mesh.shape["feat"]),
        mesh=mesh, in_specs=in_specs, out_specs=out_specs, check_vma=False,
    )
```

```python
import functools
import math

import jax
import jax.numpy as jnp
import ml_dtypes
import numpy as np
from jax import lax
from jax.experimental import pallas as pl
from jax.experimental.pallas import tpu as pltpu
from jax.sharding import PartitionSpec as P

TILE = 128
GROUP = 4
DECAY = 0.9
RATE = 8.0
BF16 = jnp.bfloat16
F32 = jnp.float32
MESH = pl.DeviceIdType.MESH


def cosine_basis():
    k = np.arange(TILE)[:, None].astype(np.float64)
    n = np.arange(TILE)[None, :].astype(np.float64)
    scale = np.where(k == 0, math.sqrt(1.0 / TILE), math.sqrt(2.0 / TILE))
    return scale * np.cos(math.pi * (2.0 * n + 1.0) * k / (2.0 * TILE))


def dot(a, b):
    return jnp.dot(a, b, preferred_element_type=F32)


def dot_nt(a, b):
    return lax.dot_general(a, b, (((1,), (1,)), ((), ())), preferred_element_type=F32)


def encode_kernel(nq, m_ref, g_ref, s_ref, basis_ref, basis_t_ref, out_ref, pv_ref, so_ref):
    step = pl.program_id(0)
    cols = m_ref.shape[2]
    ctiles = s_ref.shape[2]
    keep = s_ref.shape[3]
    per = keep * ctiles
    lane = lax.broadcasted_iota(jnp.int32, (ctiles, TILE), 1)

    @pl.when(step == 0)
    def _():
        so_ref[...] = jnp.zeros_like(so_ref)

    marks = []
    listed = so_ref[...]
    for i in range(GROUP):
        chosen = s_ref[0, i]
        for k in range(keep):
            wide = jnp.broadcast_to(chosen[:, k : k + 1], (ctiles, TILE))
            marks.append((wide == lane).astype(F32))
            listed = jnp.where(lane == (step * GROUP + i) * keep + k, wide.astype(F32), listed)
    so_ref[...] = listed
    onehot = jnp.concatenate(marks, axis=0).astype(BF16)
    rows = dot(onehot, basis_ref[...]).astype(BF16)
    rows_t = dot_nt(basis_t_ref[...], onehot).astype(BF16)

    row_id = lax.broadcasted_iota(jnp.int32, (per, cols), 0)
    col_id = lax.broadcasted_iota(jnp.int32, (per, cols), 1)
    own_tile = (row_id & (ctiles - 1)) == (col_id >> 7)
    kept = []
    for i in range(GROUP):
        at = slice(i * TILE, (i + 1) * TILE)
        chosen_rows = rows[i * per : (i + 1) * per]
        part = DECAY * dot(chosen_rows, m_ref[0, at]) + dot(chosen_rows, g_ref[0, at])
        kept.append(jnp.where(own_tile, part, 0.0).astype(BF16))
    kept = jnp.concatenate(kept, axis=0)

    fold_r = lax.broadcasted_iota(jnp.int32, (GROUP * keep, GROUP * per), 0)
    fold_c = lax.broadcasted_iota(jnp.int32, (GROUP * keep, GROUP * per), 1)
    fold = (fold_r == fold_c // ctiles).astype(F32).astype(BF16)
    compact = dot(fold, kept).astype(BF16)
    for c in range(ctiles):
        owner, q = c // nq, c % nq
        pv_ref[(owner // 2) * nq + q, owner % 2] = compact[:, c * TILE : (c + 1) * TILE]

    own_lane = lax.broadcasted_iota(jnp.int32, (TILE, GROUP * per), 1) // per
    for i in range(GROUP):
        at = slice(i * TILE, (i + 1) * TILE)
        blended = DECAY * m_ref[0, at].astype(F32) + g_ref[0, at].astype(F32)
        lhs = jnp.where(own_lane == i, rows_t, jnp.zeros_like(rows_t))
        out_ref[0, at] = (blended - dot(lhs, kept)).astype(BF16)


def mix_kernel(
    xs_n, ys_n, zs_n, nq, scale, feature_scale,
    pv_ref, so_ref, w_ref, t_ref, basis_t_ref,
    wout_ref, proj_ref,
    gat, selg, ohs, bsel, wv, tv, wo, own, cs, cr, xsend, xr,
    w_sem, t_sem, wo_sem, loc_sem, ag_send, ag_recv, c_send, c_recv, x_send, x_recv,
):
    feat, work = lax.axis_index("feat"), lax.axis_index("work")
    x, core = feat // 2, feat % 2
    z, y = work // ys_n, work % ys_n
    workers = ys_n * zs_n
    steps = xs_n * nq
    ak = gat.shape[3]
    groups = ak // 16
    span = workers * 16
    tokens = tv.shape[0]
    half = tokens // 2
    width = GROUP * TILE

    def zpeer(d):
        return lax.rem(z + d, zs_n) * ys_n + y

    def ypeer(d):
        return z * ys_n + lax.rem(y + d, ys_n)

    other_core = x * 2 + 1 - core

    def xpeer(d):
        return lax.rem(x + d, xs_n) * 2 + core

    def owner_x(s):
        return lax.rem(x + 1 + s // nq, xs_n)

    def tile_of(s, h):
        cc = core if h == 0 else 1 - core
        return (owner_x(s) * 2 + cc) * nq + s % nq

    loads = []
    for s in range(steps):
        for h in range(2):
            off = pl.multiple_of(tile_of(s, h) * TILE, TILE)
            loads.append(
                pltpu.make_async_copy(w_ref.at[:, pl.ds(off, TILE)], wv.at[s, h], w_sem.at[s, h])
            )
    load_t = pltpu.make_async_copy(t_ref, tv, t_sem.at[0])
    for s in range(steps + 1):
        src = so_ref if s == 0 else pv_ref.at[owner_x(s - 1) * nq + (s - 1) % nq]
        dst = selg.at[work] if s == 0 else gat.at[s - 1, work]
        pltpu.make_async_copy(src, dst, loc_sem.at[s]).start()

    barrier = pltpu.get_barrier_semaphore()
    count = 0
    for d in range(1, zs_n):
        pl.semaphore_signal(barrier, inc=1, device_id={"work": zpeer(d)}, device_id_type=MESH)
        count += 1
    for d in range(1, ys_n):
        pl.semaphore_signal(barrier, inc=1, device_id={"work": ypeer(d)}, device_id_type=MESH)
        count += 1
    pl.semaphore_signal(barrier, inc=1, device_id={"feat": other_core}, device_id_type=MESH)
    count += 1
    for d in range(1, xs_n):
        pl.semaphore_signal(barrier, inc=1, device_id={"feat": xpeer(d)}, device_id_type=MESH)
        count += 1
    pl.semaphore_wait(barrier, count)

    def source(r):
        return so_ref if r == 0 else pv_ref.at[owner_x(r - 1) * nq + (r - 1) % nq]

    def slot(r, w):
        return selg.at[w] if r == 0 else gat.at[r - 1, w]

    sent = []

    def push(r, src, w, to, which):
        copy = pltpu.make_async_remote_copy(
            src_ref=src, dst_ref=slot(r, w),
            send_sem=ag_send.at[r, which], recv_sem=ag_recv.at[r, w],
            device_id={"work": to}, device_id_type=MESH,
        )
        copy.start()
        sent.append(copy)

    def arrived(r, w):
        pltpu.make_async_remote_copy(
            src_ref=slot(r, w), dst_ref=slot(r, w),
            send_sem=ag_send.at[r, 0], recv_sem=ag_recv.at[r, w],
            device_id={"work": work}, device_id_type=MESH,
        ).wait_recv()

    def push_own(r):
        for d in range(1, zs_n):
            push(r, source(r), work, zpeer(d), d - 1)
        for e in range(1, ys_n):
            push(r, source(r), work, ypeer(e), zs_n - 1 + e - 1)

    def forward(r):
        base = zs_n - 1 + ys_n - 1
        for d in range(1, zs_n):
            w = zpeer(d)
            arrived(r, w)
            for e in range(1, ys_n):
                push(r, slot(r, w), w, ypeer(e), base + (d - 1) * (ys_n - 1) + e - 1)
        if r + 2 <= steps:
            push_own(r + 2)

    def rest(r):
        for e in range(1, ys_n):
            for d in range(zs_n):
                arrived(r, lax.rem(z + d, zs_n) * ys_n + lax.rem(y + e, ys_n))
        pltpu.make_async_copy(source(r), slot(r, work), loc_sem.at[r]).wait()

    push_own(0)
    push_own(1)
    for copy in loads:
        copy.start()
    load_t.start()
    forward(0)
    rest(0)

    ctiles = selg.shape[1]
    table = selg[...].reshape(workers * ctiles, TILE)
    fill = -table.shape[0] % TILE
    if fill:
        table = jnp.concatenate([table, jnp.zeros((fill, TILE), F32)], axis=0)
    table = table.T[:ak]
    lane = lax.broadcasted_iota(jnp.int32, (ak, TILE), 1).astype(F32)
    for w in range(workers):
        for c in range(ctiles):
            at = w * ctiles + c
            wide = jnp.broadcast_to(table[:, at : at + 1], (ak, TILE))
            hot = (wide == lane).astype(F32).astype(BF16)
            ohs[c, :, w * 16 : (w + 1) * 16, :] = hot.reshape(groups, 16, TILE)
    forward(1)
    for c in range(ctiles):
        for g in range(groups):
            bsel[c, g] = dot_nt(basis_t_ref[...], ohs[c, g]).astype(BF16)

    part_of = (lax.broadcasted_iota(jnp.int32, (TILE, span), 1) >> 2) & (GROUP - 1)

    def decode(s):
        for h in range(2):
            cc = core if h == 0 else 1 - core
            c = tile_of(s, h)
            loads[s * 2 + h].wait()

            def body(g, carry):
                r16 = pl.multiple_of(g * 16, 16)
                rw = pl.multiple_of(g * width, width)
                values = gat[s, :, cc, pl.ds(r16, 16), :].reshape(span, TILE)
                vectors = bsel[c, g]
                lhs = jnp.concatenate(
                    [jnp.where(part_of == i, vectors, jnp.zeros_like(vectors)) for i in range(GROUP)],
                    axis=0,
                )
                update = dot(lhs, values)
                fresh = wv[s, h, pl.ds(rw, width), :].astype(F32) - scale * update
                wo[s, pl.ds(rw, width), h * TILE : (h + 1) * TILE] = fresh.astype(BF16)
                return carry

            lax.fori_loop(0, groups, body, 0, unroll=True)
            out_copy(s, h).start()

    def out_copy(s, h):
        off = pl.multiple_of(tile_of(s, h) * TILE, TILE)
        return pltpu.make_async_copy(
            wo.at[s, :, h * TILE : (h + 1) * TILE], wout_ref.at[:, pl.ds(off, TILE)], wo_sem.at[s, h]
        )

    def core_copy(s, p):
        at = slice(p * half, (p + 1) * half)
        return pltpu.make_async_remote_copy(
            src_ref=cs.at[s, at], dst_ref=cr.at[s, at],
            send_sem=c_send.at[s, p], recv_sem=c_recv.at[s, p],
            device_id={"feat": other_core}, device_id_type=MESH,
        )

    def x_copy(s, p):
        d = s // nq + 1
        at = slice(p * half, (p + 1) * half)
        return pltpu.make_async_remote_copy(
            src_ref=xsend.at[s, at], dst_ref=xr.at[s, at],
            send_sem=x_send.at[s, p], recv_sem=x_recv.at[s, p],
            device_id={"feat": xpeer(d)}, device_id_type=MESH,
        )

    block = half

    def multiply(s, p):
        def body(t, carry):
            at = pl.ds(pl.multiple_of(p * half + t * block, block), block)
            both = dot(tv[at, :], wo[s])
            own[s, at, :] = both[:, :TILE]
            cs[s, at, :] = both[:, TILE:].astype(BF16)
            return carry

        lax.fori_loop(0, half // block, body, 0)
        core_copy(s, p).start()

    away = steps - nq

    def finish(s, p):
        at = slice(p * half, (p + 1) * half)
        core_copy(s, p).wait_recv()
        xsend[s, at] = (own[s, at] + cr[s, at].astype(F32)).astype(BF16)
        x_copy(s, p).start()

    for s in range(steps):
        rest(s + 1)
        if s == 0:
            forward(2)
        decode(s)
        if s == 0:
            load_t.wait()
        multiply(s, 0)
        if s + 3 <= steps:
            forward(s + 3)
        multiply(s, 1)
        if s < away:
            for p in range(2):
                finish(s, p)

    for q in range(nq):
        s = away + q
        for p in range(2):
            at = slice(p * half, (p + 1) * half)
            core_copy(s, p).wait_recv()
            total = own[s, at] + cr[s, at].astype(F32)
            for d in range(xs_n - 1):
                x_copy(d * nq + q, p).wait_recv()
                total = total + xr[d * nq + q, at].astype(F32)
            proj_ref[at, q * TILE : (q + 1) * TILE] = (total * feature_scale).astype(BF16)

    for copy in sent:
        copy.wait_send()
    for s in range(steps):
        for p in range(2):
            core_copy(s, p).wait_send()
            if s < away:
                x_copy(s, p).wait_send()
        for h in range(2):
            out_copy(s, h).wait()


def local(feats, momentum, gradient, weight, tokens, select):
    workers = lax.axis_size("work")
    rows, cols = weight.shape
    row_tiles, ctiles, keep = select.shape[1:]
    nq = ctiles // feats
    xs_n = feats // 2
    ys_n = xs_n if workers % xs_n == 0 else 1
    zs_n = workers // ys_n
    steps = xs_n * nq
    ak = row_tiles * keep
    count = tokens.shape[0]
    basis = cosine_basis()
    basis_c = jnp.asarray(basis.astype(ml_dtypes.bfloat16))
    basis_t = jnp.asarray(np.ascontiguousarray(basis.T).astype(ml_dtypes.bfloat16))
    height = GROUP * TILE

    moment_out, values, listed = pl.pallas_call(
        functools.partial(encode_kernel, nq),
        grid=(row_tiles // GROUP,),
        in_specs=[
            pl.BlockSpec((1, height, cols), lambda g: (0, g, 0)),
            pl.BlockSpec((1, height, cols), lambda g: (0, g, 0)),
            pl.BlockSpec((1, GROUP, ctiles, keep), lambda g: (0, g, 0, 0)),
            pl.BlockSpec((TILE, TILE), lambda g: (0, 0)),
            pl.BlockSpec((TILE, TILE), lambda g: (0, 0)),
        ],
        out_specs=[
            pl.BlockSpec((1, height, cols), lambda g: (0, g, 0)),
            pl.BlockSpec((steps, 2, 16, TILE), lambda g: (0, 0, g, 0)),
            pl.BlockSpec((ctiles, TILE), lambda g: (0, 0)),
        ],
        out_shape=[
            jax.ShapeDtypeStruct(momentum.shape, BF16),
            jax.ShapeDtypeStruct((steps, 2, ak, TILE), BF16),
            jax.ShapeDtypeStruct((ctiles, TILE), F32),
        ],
        compiler_params=pltpu.CompilerParams(vmem_limit_bytes=58 * 1024 * 1024),
        cost_estimate=pl.CostEstimate(flops=4 * rows * cols * 160, bytes_accessed=6 * rows * cols, transcendentals=0),
        name="encode",
    )(momentum, gradient, select, basis_c, basis_t)

    sends = (zs_n - 1) + zs_n * (ys_n - 1)
    away = steps - nq
    dma = pltpu.SemaphoreType.DMA
    anywhere = pl.BlockSpec(memory_space=pl.ANY)
    vmem = pl.BlockSpec(memory_space=pltpu.VMEM)
    hbm = pl.BlockSpec(memory_space=pltpu.HBM)
    weight_out, projected = pl.pallas_call(
        functools.partial(
            mix_kernel, xs_n, ys_n, zs_n, nq, RATE / workers, 1.0 / math.sqrt(rows * feats)
        ),
        in_specs=[anywhere, anywhere, hbm, hbm, vmem],
        out_specs=[anywhere, vmem],
        out_shape=[
            pltpu.VMEM(weight.shape, BF16),
            jax.ShapeDtypeStruct((count, cols // feats), BF16),
        ],
        scratch_shapes=[
            pltpu.VMEM((steps, workers, 2, ak, TILE), BF16),
            pltpu.VMEM((workers, ctiles, TILE), F32),
            pltpu.VMEM((ctiles, ak // 16, workers * 16, TILE), BF16),
            pltpu.VMEM((ctiles, ak // 16, TILE, workers * 16), BF16),
            pltpu.VMEM((steps, 2, rows, TILE), BF16),
            pltpu.VMEM((count, rows), BF16),
            pltpu.VMEM((steps, rows, 2 * TILE), BF16),
            pltpu.VMEM((steps, count, TILE), F32),
            pltpu.VMEM((steps, count, TILE), BF16),
            pltpu.VMEM((steps, count, TILE), BF16),
            pltpu.VMEM((away, count, TILE), BF16),
            pltpu.VMEM((away, count, TILE), BF16),
            dma((steps, 2)),
            dma((1,)),
            dma((steps, 2)),
            dma((steps + 1,)),
            dma((steps + 1, sends)),
            dma((steps + 1, workers)),
            dma((steps, 2)),
            dma((steps, 2)),
            dma((away, 2)),
            dma((away, 2)),
        ],
        compiler_params=pltpu.CompilerParams(
            collective_id=0, has_side_effects=True, vmem_limit_bytes=58 * 1024 * 1024
        ),
        cost_estimate=pl.CostEstimate(
            flops=2 * count * rows * cols, bytes_accessed=20 * 1024 * 1024, transcendentals=0
        ),
        name="mix",
    )(values, listed, weight, tokens, basis_t)
    return (moment_out, weight_out, projected)


def solution(mesh):
    in_specs = (
        P("work", "feat", None),
        P("work", "feat", None),
        P("feat", None),
        P("work", "feat"),
        P("work", "feat", None, None),
    )
    out_specs = (P("work", "feat", None), P("feat", None), P("work", "feat"))
    return jax.shard_map(
        functools.partial(local, mesh.shape["feat"]),
        mesh=mesh, in_specs=in_specs, out_specs=out_specs, check_vma=False,
    )
```
